32 devices in a mesh: ctx: 8 (over z, x), ch: 4 (over y, core).
Axes of the slice: x: 2, y: 2, z: 4, core: 2. Of those that a mesh axis runs over, the one named last changes fastest.
Arguments:
- proj: bfloat16 [3, 1024, 4096], P(None, 'ctx', 'ch'), may hold values from -6 to 6
- short_filter: float32 [3, 3, 4096], P(None, None, 'ch'), may hold values from -3 to 3
- long_filter: bfloat16 [1024, 4096], P('ctx', 'ch'), may hold values from -6 to 6
- out_grad: bfloat16 [1024, 4096], P('ctx', 'ch'), may hold values from -24 to 24
- conv_out: bfloat16 [1024, 4096], P('ctx', 'ch'), may hold values from -6 to 6
Outputs:
- proj_grad: bfloat16 [3, 1024, 4096], P(None, 'ctx', 'ch')
- short_grad: float32 [3, 3, 4096], P(None, None, 'ch')
- filter_grad: float32 [1024, 4096], P('ctx', 'ch')
- grad_square: float32 [], replicated
The draws below stay inside these ranges and needn't reach their ends.
All inputs are finite; a program needn't handle non-finite values.
Results may differ from the reference program's by a relative error of at most 0.012.
Values may be sent and summed in bfloat16 or wider, within the bound.
A program may use at most 192 MiB of HBM per device.

```python
import math
import jax
import jax.numpy as jnp
from jax import lax

D = 4096
KS = 3
SEQ = 1024


def draw_out_grad(key, part):
    base_key, column_key, row_key = jax.random.split(jax.random.fold_in(key, 7), 3)
    column_place = jnp.arange(D, dtype=jnp.float32) / D
    column_log = math.log(10.0) * (0.5 * column_place + 0.5 * jax.random.uniform(column_key, (D,), dtype=jnp.float32) - 0.5)
    row_log = jax.random.uniform(row_key, (SEQ, 1), dtype=jnp.float32, minval=math.log(0.5), maxval=math.log(2.0))
    values = jax.random.truncated_normal(base_key, -4.0, 4.0, (SEQ, D), dtype=jnp.float32)
    return jnp.clip(values * jnp.exp(row_log) * jnp.exp(column_log)[None, :], -24.0, 24.0).astype(jnp.bfloat16)


def steps_of(key, extent, pieces, smallest, top_value):
    def one(dim, shards_of):
        steps = jax.random.uniform(jax.random.fold_in(jax.random.fold_in(key, 6), dim), (shards_of,), jnp.float32, smallest / len(pieces), top_value / len(pieces))
        return jnp.repeat(jnp.exp(steps), extent[dim] // shards_of).reshape((-1,) + (1,) * (len(extent) - dim - 1))

    level = one(*pieces[0])
    for cut in pieces[1:]:
        level = level * one(*cut)
    return level


def normal_values(rng, dims, spread, most, shards=(), kind=jnp.bfloat16):
    values = jax.random.normal(rng, dims, jnp.float32) * spread
    if len(shards) > 0:
        values = steps_of(rng, dims, shards, -0.22, 0.18) * values
    return jnp.clip(values, min=-most, max=most).astype(kind)


def setup_inputs(seed: int = 0) -> dict:
    arg_keys = jax.random.split(jax.random.key(seed), 6)
    return {
        "proj": normal_values(arg_keys[0], (3, SEQ, D), 1.0, 6.0, ((1, 8), (2, 4))),
        "short_filter": normal_values(arg_keys[1], (3, KS, D), 0.6, 3.0, ((2, 4),), jnp.float32),
        "long_filter": normal_values(arg_keys[2], (SEQ, D), 1.0, 6.0, ((0, 8), (1, 4))),
        "out_grad": draw_out_grad(jax.random.fold_in(arg_keys[5], 71), 0),
        "conv_out": normal_values(arg_keys[4], (SEQ, D), 1.0, 6.0, ((0, 8), (1, 4))),
    }


def delay_rows(matrix, offset):
    if offset == 0:
        return matrix
    return jnp.pad(matrix, ((offset, 0), (0, 0)))[:matrix.shape[0]]


def lead_rows(matrix, offset):
    if offset == 0:
        return matrix
    return jnp.pad(matrix, ((0, offset), (0, 0)))[offset:]


def round_trip(values):
    return lax.optimization_barrier(values.astype(jnp.bfloat16)).astype(jnp.float32)


def reference(proj, short_filter, long_filter, out_grad, conv_out):
    norm_scale = float(SEQ) ** -0.5
    padded_length = 2 * SEQ

    def block_grads(block_index):
        first_channel = (block_index * 128).astype(jnp.int32)
        streams = lax.dynamic_slice_in_dim(proj, first_channel, 128, 2).astype(jnp.float32)
        tap_block = lax.dynamic_slice_in_dim(short_filter, first_channel, 128, 2)
        filter_block = lax.dynamic_slice_in_dim(long_filter, first_channel, 128, 1).astype(jnp.float32)
        grad_block = lax.dynamic_slice_in_dim(out_grad, first_channel, 128, 1).astype(jnp.float32)
        saved_block = lax.dynamic_slice_in_dim(conv_out, first_channel, 128, 1).astype(jnp.float32)
        delayed = [[delay_rows(streams[stream], offset) for offset in range(KS)] for stream in range(3)]
        mixed = []
        for stream in range(3):
            running = tap_block[stream, 0][None, :] * delayed[stream][0]
            for offset in range(1, KS):
                running = running + tap_block[stream, offset][None, :] * delayed[stream][offset]
            mixed.append(running)
        product_u = round_trip(mixed[1] * mixed[2])
        product_g = round_trip(grad_block * mixed[0])
        spectrum_h = jnp.fft.rfft(filter_block, n=padded_length, axis=0)
        spectrum_u = jnp.fft.rfft(product_u, n=padded_length, axis=0)
        spectrum_g = jnp.fft.rfft(product_g, n=padded_length, axis=0)
        input_grad = jnp.fft.irfft(jnp.conj(spectrum_h) * spectrum_g, n=padded_length, axis=0)[:SEQ] * norm_scale
        input_grad = round_trip(input_grad)
        lag_grad = jnp.fft.irfft(jnp.conj(spectrum_u) * spectrum_g, n=padded_length, axis=0)[:SEQ] * norm_scale
        stream_grads = [grad_block * saved_block, input_grad * mixed[2], input_grad * mixed[1]]
        proj_grads = []
        tap_grads = []
        for stream in range(3):
            running = tap_block[stream, 0][None, :] * stream_grads[stream]
            for offset in range(1, KS):
                running = running + tap_block[stream, offset][None, :] * lead_rows(stream_grads[stream], offset)
            proj_grads.append(running.astype(jnp.bfloat16))
            tap_grads.append(jnp.stack([jnp.sum(stream_grads[stream] * delayed[stream][offset], axis=0) for offset in range(KS)]) * norm_scale)
        square_sum = jnp.sum(lag_grad * lag_grad)
        return jnp.stack(proj_grads), jnp.stack(tap_grads), lag_grad.astype(jnp.float32), square_sum

    block_count = D // 128
    grads_blocks, taps_blocks, lag_blocks, square_blocks = lax.map(block_grads, jnp.arange(block_count, dtype=jnp.int32))
    proj_grad = jnp.transpose(grads_blocks, (1, 2, 0, 3)).reshape(3, SEQ, D)
    short_grad = jnp.transpose(taps_blocks, (1, 2, 0, 3)).reshape(3, KS, D)
    filter_grad = jnp.transpose(lag_blocks, (1, 0, 2)).reshape(SEQ, D)
    grad_square = jnp.sum(square_blocks) / (SEQ * D)
    return proj_grad, short_grad, filter_grad, grad_square
```

```python
import functools
import math

import jax
import jax.numpy as jnp
import ml_dtypes
import numpy as np
from jax import lax
from jax.experimental import pallas as pl
from jax.experimental.pallas import tpu as pltpu
from jax.sharding import PartitionSpec as P


def to_pairs(matrix, ctx_count):
    local_rows, local_channels = matrix.shape
    channel_width = local_channels // ctx_count
    shaped = matrix.reshape(local_rows // 2, 2, ctx_count, channel_width)
    return jnp.transpose(shaped, (0, 2, 1, 3)).reshape(
        local_rows // 2, ctx_count * 2 * channel_width
    )


def from_pairs(matrix, ctx_count):
    half_rows, joined = matrix.shape
    channel_width = joined // (2 * ctx_count)
    shaped = matrix.reshape(half_rows, ctx_count, 2, channel_width)
    return jnp.transpose(shaped, (0, 2, 1, 3)).reshape(half_rows * 2, ctx_count * channel_width)


def rows_down(matrix, count):
    if count == 0:
        return matrix
    filler = jnp.zeros((count, matrix.shape[1]), matrix.dtype)
    return jnp.concatenate([filler, matrix[:-count]], axis=0)


def rows_up(matrix, count):
    if count == 0:
        return matrix
    filler = jnp.zeros((count, matrix.shape[1]), matrix.dtype)
    return jnp.concatenate([matrix[count:], filler], axis=0)


def retard(matrix, offset, channel_width):
    quotient, remainder = divmod(offset, 2)
    result = rows_down(matrix, quotient)
    if remainder:
        rolled = jnp.roll(result, channel_width, axis=1)
        first_half = lax.broadcasted_iota(jnp.int32, (1, matrix.shape[1]), 1) < channel_width
        result = jnp.where(first_half, rows_down(rolled, 1), rolled)
    return result


def advance(matrix, offset, channel_width):
    quotient, remainder = divmod(offset, 2)
    result = rows_up(matrix, quotient)
    if remainder:
        rolled = jnp.roll(result, channel_width, axis=1)
        first_half = lax.broadcasted_iota(jnp.int32, (1, matrix.shape[1]), 1) < channel_width
        result = jnp.where(first_half, rolled, rows_up(rolled, 1))
    return result


def fourier_table(count, period):
    row_index = lax.broadcasted_iota(jnp.int32, (count, count), 0)
    col_index = lax.broadcasted_iota(jnp.int32, (count, count), 1)
    exponent = row_index * col_index % period
    angle = exponent.astype(jnp.float32) * (-2.0 * math.pi / period)
    return (jnp.cos(angle), jnp.sin(angle))


def angle_pair(exponent, period):
    angle = exponent.astype(jnp.float32) * (-2.0 * math.pi / period)
    return (jnp.cos(angle), jnp.sin(angle))


def contract(form, real_table, imag_table, real_part, imag_part):
    highest = lax.Precision.HIGHEST
    first = jnp.einsum(form, real_table, real_part, precision=highest) - jnp.einsum(
        form, imag_table, imag_part, precision=highest
    )
    second = jnp.einsum(form, real_table, imag_part, precision=highest) + jnp.einsum(
        form, imag_table, real_part, precision=highest
    )
    return (first, second)


def rotate(real_part, imag_part, cosine_part, sine_part):
    return (
        real_part * cosine_part - imag_part * sine_part,
        real_part * sine_part + imag_part * cosine_part,
    )


def build_tables(radix_a, radix_b, radix_c, channel_width):
    period = radix_a * radix_b * radix_c
    shape_ab = (radix_a, radix_b, 1, 1)
    digit_ka = lax.broadcasted_iota(jnp.int32, shape_ab, 0)
    digit_sb = lax.broadcasted_iota(jnp.int32, shape_ab, 1)
    turn_ab = angle_pair(radix_c * digit_sb * digit_ka % period, period)
    shape_abc = (radix_a, radix_b, radix_c, 1)
    lower_k = lax.broadcasted_iota(jnp.int32, shape_abc, 0)
    middle_k = lax.broadcasted_iota(jnp.int32, shape_abc, 1)
    digit_sc = lax.broadcasted_iota(jnp.int32, shape_abc, 2)
    turn_bc = angle_pair(digit_sc * (lower_k + radix_a * middle_k) % period, period)
    whole_k = lower_k + radix_a * middle_k + radix_a * radix_b * digit_sc
    half_cos, half_sin = angle_pair(whole_k, 2 * period)
    first_half = lax.broadcasted_iota(jnp.int32, (1, 1, 1, 2 * channel_width), 3) < channel_width
    turn_half = (jnp.where(first_half, 1.0, half_cos), jnp.where(first_half, 0.0, half_sin))
    sign_vector = jnp.where(first_half, 1.0, -1.0)
    return (
        fourier_table(radix_a, radix_a),
        fourier_table(radix_b, radix_b),
        fourier_table(radix_c, radix_c),
        turn_ab,
        turn_bc,
        turn_half,
        sign_vector,
    )


def butterfly(values, sign_vector, channel_width):
    return sign_vector * values + jnp.roll(values, channel_width, axis=3)


def forward(signal, tables, radix_a, radix_b, radix_c, channel_width):
    table_a, table_b, table_c, turn_ab, turn_bc, turn_half, sign_vector = tables
    half_a = radix_a // 2
    values = signal.astype(jnp.float32).reshape(half_a, radix_b, radix_c, 2 * channel_width)
    highest = lax.Precision.HIGHEST
    real_part = jnp.einsum("ka,abcz->kbcz", table_a[0][:, :half_a], values, precision=highest)
    imag_part = jnp.einsum("ka,abcz->kbcz", table_a[1][:, :half_a], values, precision=highest)
    real_part, imag_part = rotate(real_part, imag_part, turn_ab[0], turn_ab[1])
    real_part, imag_part = contract("kb,abcz->akcz", table_b[0], table_b[1], real_part, imag_part)
    real_part, imag_part = rotate(real_part, imag_part, turn_bc[0], turn_bc[1])
    real_part, imag_part = contract("kc,abcz->abkz", table_c[0], table_c[1], real_part, imag_part)
    real_part, imag_part = rotate(real_part, imag_part, turn_half[0], turn_half[1])
    return (
        butterfly(real_part, sign_vector, channel_width),
        butterfly(imag_part, sign_vector, channel_width),
    )


def inverse(real_part, imag_part, tables, radix_a, radix_b, radix_c, channel_width):
    table_a, table_b, table_c, turn_ab, turn_bc, turn_half, sign_vector = tables
    half_a = radix_a // 2
    real_part = butterfly(real_part, sign_vector, channel_width)
    imag_part = butterfly(imag_part, sign_vector, channel_width)
    real_part, imag_part = rotate(real_part, imag_part, turn_half[0], -turn_half[1])
    real_part, imag_part = contract("kc,abcz->abkz", table_c[0], -table_c[1], real_part, imag_part)
    real_part, imag_part = rotate(real_part, imag_part, turn_bc[0], -turn_bc[1])
    real_part, imag_part = contract("kb,abcz->akcz", table_b[0], -table_b[1], real_part, imag_part)
    real_part, imag_part = rotate(real_part, imag_part, turn_ab[0], -turn_ab[1])
    real_part, imag_part = contract(
        "ka,abcz->kbcz", table_a[0][:half_a, :], -table_a[1][:half_a, :], real_part, imag_part
    )
    half_rows = half_a * radix_b * radix_c
    return (
        real_part.reshape(half_rows, 2 * channel_width),
        imag_part.reshape(half_rows, 2 * channel_width),
    )


def spectral(filter_pairs, product_u, product_g, ctx_count, local_rows):
    channel_width = filter_pairs.shape[1] // 2
    radix_b = local_rows // 16
    radix_c = 16
    sequence_length = ctx_count * local_rows
    tables = build_tables(ctx_count, radix_b, radix_c, channel_width)
    filter_real, filter_imag = forward(
        filter_pairs, tables, ctx_count, radix_b, radix_c, channel_width
    )
    gated_real, gated_imag = forward(product_u, tables, ctx_count, radix_b, radix_c, channel_width)
    grad_real, grad_imag = forward(product_g, tables, ctx_count, radix_b, radix_c, channel_width)
    input_real = filter_real * grad_real + filter_imag * grad_imag
    input_imag = filter_real * grad_imag - filter_imag * grad_real
    lag_real = gated_real * grad_real + gated_imag * grad_imag
    lag_imag = gated_real * grad_imag - gated_imag * grad_real
    joint_real, joint_imag = inverse(
        input_real - lag_imag,
        input_imag + lag_real,
        tables,
        ctx_count,
        radix_b,
        radix_c,
        channel_width,
    )
    final_scale = 1.0 / (2.0 * sequence_length * math.sqrt(sequence_length))
    return ((joint_real * final_scale).astype(jnp.bfloat16), joint_imag * final_scale)


def shards(proj, short_filter, long_filter, out_grad, conv_out):
    ctx_count = lax.axis_size("ctx")
    local_rows, local_channels = long_filter.shape
    tap_count = short_filter.shape[1]
    channel_width = local_channels // ctx_count
    sequence_length = local_rows * ctx_count
    norm_scale = float(sequence_length) ** (-0.5)
    arrived = (
        lax.all_to_all(
            to_pairs(proj[0], ctx_count), "ctx", split_axis=1, concat_axis=0, tiled=True
        ),
        lax.all_to_all(
            to_pairs(proj[1], ctx_count), "ctx", split_axis=1, concat_axis=0, tiled=True
        ),
        lax.all_to_all(
            to_pairs(proj[2], ctx_count), "ctx", split_axis=1, concat_axis=0, tiled=True
        ),
        lax.all_to_all(
            to_pairs(long_filter, ctx_count), "ctx", split_axis=1, concat_axis=0, tiled=True
        ),
        lax.all_to_all(
            to_pairs(out_grad, ctx_count), "ctx", split_axis=1, concat_axis=0, tiled=True
        ),
        lax.all_to_all(
            to_pairs(conv_out, ctx_count), "ctx", split_axis=1, concat_axis=0, tiled=True
        ),
    )
    streams = [
        arrived[0].astype(jnp.float32),
        arrived[1].astype(jnp.float32),
        arrived[2].astype(jnp.float32),
    ]
    filter_pairs = arrived[3]
    grad_pairs = arrived[4].astype(jnp.float32)
    saved_pairs = arrived[5].astype(jnp.float32)
    local_taps = lax.dynamic_slice_in_dim(
        short_filter, lax.axis_index("ctx") * channel_width, channel_width, 2
    )
    local_taps = jnp.concatenate([local_taps, local_taps], axis=2)
    delayed = [
        [retard(streams[stream], offset, channel_width) for offset in range(tap_count)]
        for stream in range(3)
    ]
    mixed = []
    for stream in range(3):
        running = local_taps[stream, 0][None, :] * delayed[stream][0]
        for offset in range(1, tap_count):
            running = running + local_taps[stream, offset][None, :] * delayed[stream][offset]
        mixed.append(running)
    product_u = (mixed[1] * mixed[2]).astype(jnp.bfloat16)
    product_g = (grad_pairs * mixed[0]).astype(jnp.bfloat16)
    input_pairs, lag_pairs = spectral(filter_pairs, product_u, product_g, ctx_count, local_rows)
    input_values = input_pairs.astype(jnp.float32)
    stream_grads = [grad_pairs * saved_pairs, input_values * mixed[2], input_values * mixed[1]]
    outgoing = []
    tap_sums = []
    for stream in range(3):
        running = local_taps[stream, 0][None, :] * stream_grads[stream]
        for offset in range(1, tap_count):
            running = running + local_taps[stream, offset][None, :] * advance(
                stream_grads[stream], offset, channel_width
            )
        outgoing.append(running.astype(jnp.bfloat16))
        column_sums = []
        for offset in range(tap_count):
            column_total = jnp.sum(stream_grads[stream] * delayed[stream][offset], axis=0)
            column_sums.append(column_total[:channel_width] + column_total[channel_width:])
        tap_sums.append(jnp.stack(column_sums))
    returned = (
        lax.all_to_all(outgoing[0], "ctx", split_axis=0, concat_axis=1, tiled=True),
        lax.all_to_all(outgoing[1], "ctx", split_axis=0, concat_axis=1, tiled=True),
        lax.all_to_all(outgoing[2], "ctx", split_axis=0, concat_axis=1, tiled=True),
    )
    proj_grad = jnp.stack(
        [
            from_pairs(returned[0], ctx_count),
            from_pairs(returned[1], ctx_count),
            from_pairs(returned[2], ctx_count),
        ]
    )
    short_grad = lax.all_gather(jnp.stack(tap_sums), "ctx", axis=2, tiled=True) * norm_scale
    filter_grad = from_pairs(
        lax.all_to_all(lag_pairs, "ctx", split_axis=0, concat_axis=1, tiled=True), ctx_count
    )
    square_total = lax.psum(jnp.sum(filter_grad * filter_grad), ("ctx", "ch"))
    grad_square = square_total / float(sequence_length * local_channels * lax.axis_size("ch"))
    return (proj_grad, short_grad, filter_grad, grad_square)


LANES = 128
HALO = 8
MESH = pl.DeviceIdType.MESH
H, G, U, DU, LAG, PART, FINAL, SQUARE = range(8)


def real_tables(length):
    period = 2 * length
    k = np.arange(length, dtype=np.int64)[:, None]
    t = np.arange(length, dtype=np.int64)[None, :]
    angle = (k * t % period) * (2.0 * np.pi / period)
    sine = np.sin(angle)
    sine[0] = 1.0 - 2.0 * (np.arange(length) % 2)
    table = np.concatenate([np.cos(angle), sine], axis=0)
    return table.astype(ml_dtypes.bfloat16), np.ascontiguousarray(table.T).astype(ml_dtypes.bfloat16)


def fused_kernel(
    n,
    heads,
    proj,
    taps,
    long_filter,
    out_grad,
    conv_out,
    table_hbm,
    inverse_hbm,
    proj_grad,
    short_grad,
    filter_grad,
    square,
    table,
    inverse,
    halo_down,
    halo_up,
    from_prev,
    from_next,
    ext,
    mixed,
    gate,
    send_g,
    send_u,
    got_h,
    got_g,
    got_u,
    spectrum,
    product,
    du_all,
    lag_all,
    got_du,
    got_lag,
    part,
    got_part,
    final,
    got_final,
    total_ctx,
    got_ctx,
    total_ch,
    got_ch,
    send_sem,
    recv_sem,
    halo_sem,
    head_sem,
    table_sem,
):
    me = lax.axis_index("ctx")
    head = lax.axis_index("ch")
    rows = long_filter.shape[0]
    length = n * rows
    taps_count = taps.shape[1]
    norm = float(length) ** -0.5
    prev, following = lax.rem(me + n - 1, n), lax.rem(me + 1, n)

    def lanes(index):
        return pl.ds(pl.multiple_of(index * LANES, LANES), LANES)

    def block(index, size=rows):
        return pl.ds(pl.multiple_of(index * rows, rows), size)

    def send(kind, peer, source, target):
        return pltpu.make_async_remote_copy(
            src_ref=source,
            dst_ref=target,
            send_sem=send_sem.at[kind, peer],
            recv_sem=recv_sem.at[kind, me],
            device_id=(peer, head),
            device_id_type=MESH,
        )

    def arrive(kind, peer, target):
        pltpu.make_async_remote_copy(
            src_ref=target,
            dst_ref=target,
            send_sem=send_sem.at[kind, peer],
            recv_sem=recv_sem.at[kind, peer],
            device_id=(peer, head),
            device_id_type=MESH,
        ).wait_recv()

    def peers(body):
        def step(i, carry):
            body(lax.rem(me + i, n))
            return carry

        lax.fori_loop(1, n, step, 0)

    barrier = pltpu.get_barrier_semaphore()
    for i in range(1, n):
        pl.semaphore_signal(
            barrier, inc=1, device_id=(lax.rem(me + i, n), head), device_id_type=MESH
        )
    for i in range(1, heads):
        pl.semaphore_signal(
            barrier, inc=1, device_id=(me, lax.rem(head + i, heads)), device_id_type=MESH
        )
    load_table = pltpu.make_async_copy(table_hbm, table, table_sem.at[0])
    load_inverse = pltpu.make_async_copy(inverse_hbm, inverse, table_sem.at[1])
    load_table.start()
    load_inverse.start()

    row = lax.broadcasted_iota(jnp.int32, (16, proj.shape[2]), 0)

    def pack(parts):
        packed = jnp.zeros(row.shape, jnp.float32)
        for place, (values, first) in enumerate(parts):
            shift = (2 * place - first) % 16
            moved = pltpu.roll(values.astype(jnp.float32), shift, 0) if shift else values.astype(jnp.float32)
            packed = jnp.where((row >= 2 * place) & (row < 2 * place + 2), moved, packed)
        return packed.astype(jnp.bfloat16)

    halo_down[...] = pack([(proj[j, rows - 16 : rows, :], 14) for j in range(3)])
    halo_up[...] = pack(
        [(proj[j, 0:16, :], 0) for j in range(3)] + [(out_grad[0:16, :], 0), (conv_out[0:16, :], 0)]
    )
    pl.semaphore_wait(barrier, n - 1 + heads - 1)

    def halo(source, target, index, peer):
        return pltpu.make_async_remote_copy(
            src_ref=source,
            dst_ref=target,
            send_sem=halo_sem.at[0, index],
            recv_sem=halo_sem.at[1, index],
            device_id=(peer, head),
            device_id_type=MESH,
        )

    down = halo(halo_down, from_prev, 0, following)
    up = halo(halo_up, from_next, 1, prev)
    down.start()
    up.start()

    def send_filter(peer):
        return send(H, peer, long_filter.at[:, lanes(peer)], got_h.at[block(me), :])

    peers(lambda peer: send_filter(peer).start())
    got_h[block(me), :] = long_filter[:, lanes(me)]
    part[...] = jnp.zeros_like(part)
    du_all[length : length + 16, :] = jnp.zeros((16, LANES), jnp.bfloat16)
    for j in range(3):
        ext[j, HALO : HALO + rows, :] = proj[j].astype(jnp.float32)
    ext[3, 0:rows, :] = out_grad[...].astype(jnp.float32) * conv_out[...].astype(jnp.float32)

    down.wait_recv()
    up.wait_recv()
    before = jnp.where(me == 0, 0.0, from_prev[...].astype(jnp.float32))
    after = jnp.where(me == n - 1, 0.0, from_next[...].astype(jnp.float32))
    for j in range(3):
        ext[j, 0:HALO, :] = pltpu.roll(before, (6 - 2 * j) % 16, 0)[0:8, :]
        ext[j, HALO + rows : 2 * HALO + rows, :] = (pltpu.roll(after, 16 - 2 * j, 0) if j else after)[0:8, :]
    ext[3, rows : rows + HALO, :] = (
        pltpu.roll(after, 10, 0)[0:8, :] * pltpu.roll(after, 8, 0)[0:8, :]
    )

    def gates(peer):
        at = lanes(peer)
        values = []
        for j in range(3):
            running = taps[j, 0:1, at] * ext[j, HALO : 2 * HALO + rows, at]
            for m in range(1, taps_count):
                running = running + taps[j, m : m + 1, at] * ext[j, HALO - m : 2 * HALO + rows - m, at]
            values.append(running)
        mixed[0, :, at] = values[1]
        mixed[1, :, at] = values[2]
        u = (values[1][:rows] * values[2][:rows]).astype(jnp.bfloat16)
        g = (out_grad[:, at].astype(jnp.float32) * values[0][:rows]).astype(jnp.bfloat16)
        return g, u

    def send_grad(peer):
        return send(G, peer, send_g.at[peer], got_g.at[block(me), :])

    def send_input(peer):
        return send(U, peer, send_u.at[peer], got_u.at[block(me), :])

    def gate_peer(peer):
        g, u = gates(peer)
        send_g[peer] = g
        send_u[peer] = u
        send_grad(peer).start()

    peers(gate_peer)
    peers(lambda peer: send_input(peer).start())
    g, u = gates(me)
    got_g[block(me), :] = g
    got_u[block(me), :] = u

    def stream(j, at, index, read):
        running = taps[j, 0:1, at] * read(0)
        for m in range(1, taps_count):
            running = running + taps[j, m : m + 1, at] * read(m)
        proj_grad[j, :, at] = running.astype(jnp.bfloat16)
        for m in range(taps_count):
            part[index, j * taps_count + m : j * taps_count + m + 1, :] = jnp.sum(
                read(0) * ext[j, HALO - m : HALO + rows - m, at], axis=0, keepdims=True
            )

    def first_stream(index, carry):
        at = lanes(index)
        stream(0, at, index, lambda m: ext[3, m : m + rows, at])
        return carry

    lax.fori_loop(0, n, first_stream, 0)

    step_rows = min(256, length)

    def transform(slot, source):
        def tile(i, carry):
            at = pl.ds(pl.multiple_of(i * step_rows, step_rows), step_rows)
            spectrum[slot, at, :] = jnp.dot(
                table[at, :], source[...], preferred_element_type=jnp.float32
            )
            return carry

        lax.fori_loop(0, 2 * length // step_rows, tile, 0)

    def correlate(slot):
        def tile(i, carry):
            low = pl.ds(pl.multiple_of(i * step_rows, step_rows), step_rows)
            high = pl.ds(pl.multiple_of(length + i * step_rows, step_rows), step_rows)
            a_cos, a_sin = spectrum[slot, low, :], spectrum[slot, high, :]
            g_cos, g_sin = spectrum[1, low, :], spectrum[1, high, :]
            edge = lax.broadcasted_iota(jnp.int32, (step_rows, LANES), 0) + i * step_rows == 0
            cos_cos, sin_sin = a_cos * g_cos, a_sin * g_sin
            product[low, :] = jnp.where(edge, 0.5 * cos_cos, cos_cos + sin_sin).astype(jnp.bfloat16)
            product[high, :] = jnp.where(
                edge, 0.5 * sin_sin, a_cos * g_sin - a_sin * g_cos
            ).astype(jnp.bfloat16)
            return carry

        lax.fori_loop(0, length // step_rows, tile, 0)

    def invert(store, start):
        def tile(i, carry):
            at = pl.ds(pl.multiple_of(i * step_rows, step_rows), step_rows)
            values = jnp.dot(inverse[at, :], product[...], preferred_element_type=jnp.float32)
            return store(at, values * (norm / length), carry)

        return lax.fori_loop(0, length // step_rows, tile, start)

    load_table.wait()
    peers(lambda peer: arrive(H, peer, got_h.at[block(peer), :]))
    transform(0, got_h)
    peers(lambda peer: arrive(G, peer, got_g.at[block(peer), :]))
    transform(1, got_g)
    correlate(0)
    load_inverse.wait()

    def store_du(at, values, carry):
        du_all[at, :] = values.astype(jnp.bfloat16)
        return carry

    invert(store_du, 0)

    def send_du(peer):
        return send(DU, peer, du_all.at[block(peer, rows + 16), :], got_du.at[me])

    peers(lambda peer: send_du(peer).start())
    got_du[me] = du_all[block(me, rows + 16), :]

    peers(lambda peer: arrive(U, peer, got_u.at[block(peer), :]))
    transform(2, got_u)
    correlate(2)

    def store_lag(at, values, carry):
        lag_all[at, :] = values.astype(jnp.bfloat16)
        return carry + jnp.sum((values * values).reshape(step_rows // 8, 8, LANES), axis=0)

    total_ctx[...] = invert(store_lag, jnp.zeros((8, LANES), jnp.float32))

    def send_square(peer):
        return send(SQUARE, peer, total_ctx, got_ctx.at[me])

    def send_lag(peer):
        return send(LAG, peer, lag_all.at[block(peer), :], got_lag.at[me])

    peers(lambda peer: send_square(peer).start())
    peers(lambda peer: send_lag(peer).start())

    def send_part(peer):
        return send(PART, peer, part.at[peer], got_part.at[me])

    def rest(index):
        at = lanes(index)
        du = got_du[index].astype(jnp.float32)[: rows + HALO]
        gate[0] = du * mixed[1, :, at]
        gate[1] = du * mixed[0, :, at]
        stream(1, at, index, lambda m: gate[0, m : m + rows, :])
        stream(2, at, index, lambda m: gate[1, m : m + rows, :])

    def rest_peer(peer):
        arrive(DU, peer, got_du.at[peer])
        rest(peer)
        send_part(peer).start()

    rest(me)
    peers(rest_peer)

    total = total_ctx[...]
    for i in range(1, n):
        peer = lax.rem(me + i, n)
        arrive(SQUARE, peer, got_ctx.at[peer])
        total = total + got_ctx[peer]
    total_ch[...] = total

    def send_head(i):
        return pltpu.make_async_remote_copy(
            src_ref=total_ch,
            dst_ref=got_ch.at[i],
            send_sem=head_sem.at[0, i],
            recv_sem=head_sem.at[1, i],
            device_id=(me, lax.rem(head + i, heads)),
            device_id_type=MESH,
        )

    for i in range(1, heads):
        send_head(i).start()

    sums = part[me]
    for i in range(1, n):
        peer = lax.rem(me + i, n)
        arrive(PART, peer, got_part.at[peer])
        sums = sums + got_part[peer]
    final[...] = sums * norm
    got_final[me] = sums * norm

    def send_final(peer):
        return send(FINAL, peer, final, got_final.at[me])

    peers(lambda peer: send_final(peer).start())

    filter_grad[:, lanes(me)] = lag_all[block(me), :].astype(jnp.float32)

    def take_lag(peer):
        arrive(LAG, peer, got_lag.at[peer])
        filter_grad[:, lanes(peer)] = got_lag[peer].astype(jnp.float32)

    peers(take_lag)

    total = total_ch[...]
    for i in range(1, heads):
        send_head(i).wait_recv()
        total = total + got_ch[i]
    square[...] = jnp.broadcast_to(
        jnp.sum(total, keepdims=True) / float(length * n * LANES * heads), square.shape
    )

    def put_final(index):
        at = lanes(index)
        for j in range(3):
            for m in range(taps_count):
                place = j * taps_count + m
                short_grad[j, m : m + 1, at] = got_final[index, place : place + 1, :]

    def take_final(peer):
        arrive(FINAL, peer, got_final.at[peer])
        put_final(peer)

    put_final(me)
    peers(take_final)

    down.wait_send()
    up.wait_send()
    for i in range(1, heads):
        send_head(i).wait_send()

    def sent(peer):
        for one in (
            send_filter,
            send_grad,
            send_input,
            send_du,
            send_square,
            send_lag,
            send_part,
            send_final,
        ):
            one(peer).wait_send()

    peers(sent)


def fused_shards(tables, proj, short_filter, long_filter, out_grad, conv_out):
    n = lax.axis_size("ctx")
    heads = lax.axis_size("ch")
    rows, channels = long_filter.shape
    length = n * rows
    bf16, f32 = jnp.bfloat16, jnp.float32
    vmem = pl.BlockSpec(memory_space=pltpu.VMEM)
    anywhere = pl.BlockSpec(memory_space=pl.ANY)
    outs = pl.pallas_call(
        functools.partial(fused_kernel, n, heads),
        out_shape=(
            jax.ShapeDtypeStruct((3, rows, channels), bf16),
            jax.ShapeDtypeStruct(short_filter.shape, f32),
            jax.ShapeDtypeStruct((rows, channels), f32),
            jax.ShapeDtypeStruct((8, LANES), f32),
        ),
        in_specs=[vmem] * 5 + [anywhere] * 2,
        out_specs=(vmem,) * 4,
        scratch_shapes=[
            pltpu.VMEM((2 * length, length), bf16),
            pltpu.VMEM((length, 2 * length), bf16),
            pltpu.VMEM((16, channels), bf16),
            pltpu.VMEM((16, channels), bf16),
            pltpu.VMEM((16, channels), bf16),
            pltpu.VMEM((16, channels), bf16),
            pltpu.VMEM((4, rows + 2 * HALO, channels), f32),
            pltpu.VMEM((2, rows + HALO, channels), f32),
            pltpu.VMEM((2, rows + HALO, LANES), f32),
            pltpu.VMEM((n, rows, LANES), bf16),
            pltpu.VMEM((n, rows, LANES), bf16),
            pltpu.VMEM((length, LANES), bf16),
            pltpu.VMEM((length, LANES), bf16),
            pltpu.VMEM((length, LANES), bf16),
            pltpu.VMEM((3, 2 * length, LANES), f32),
            pltpu.VMEM((2 * length, LANES), bf16),
            pltpu.VMEM((length + 16, LANES), bf16),
            pltpu.VMEM((length, LANES), bf16),
            pltpu.VMEM((n, rows + 16, LANES), bf16),
            pltpu.VMEM((n, rows, LANES), bf16),
            pltpu.VMEM((n, 16, LANES), f32),
            pltpu.VMEM((n, 16, LANES), f32),
            pltpu.VMEM((16, LANES), f32),
            pltpu.VMEM((n, 16, LANES), f32),
            pltpu.VMEM((8, LANES), f32),
            pltpu.VMEM((n, 8, LANES), f32),
            pltpu.VMEM((8, LANES), f32),
            pltpu.VMEM((heads, 8, LANES), f32),
            pltpu.SemaphoreType.DMA((8, n)),
            pltpu.SemaphoreType.DMA((8, n)),
            pltpu.SemaphoreType.DMA((2, 2)),
            pltpu.SemaphoreType.DMA((2, heads)),
            pltpu.SemaphoreType.DMA((2,)),
        ],
        compiler_params=pltpu.CompilerParams(
            collective_id=0, has_side_effects=True, vmem_limit_bytes=40 * 1024 * 1024
        ),
    )(proj, short_filter, long_filter, out_grad, conv_out, *tables)
    return (outs[0], outs[1], outs[2], outs[3][0, 0])


def program(proj, short_filter, long_filter, out_grad, conv_out):
    n = lax.axis_size("ctx")
    rows, channels = long_filter.shape
    length = n * rows
    fits = (
        channels == n * LANES
        and length in (256, 512, 1024)
        and rows % 16 == 0
        and n > 2
        and short_filter.shape[1] == 3
    )
    if not fits:
        return shards(proj, short_filter, long_filter, out_grad, conv_out)
    tables = [jnp.asarray(one) for one in real_tables(length)]
    return fused_shards(tables, proj, short_filter, long_filter, out_grad, conv_out)


def solution(mesh):
    return jax.shard_map(
        program,
        mesh=mesh,
        in_specs=(
            P(None, "ctx", "ch"),
            P(None, None, "ch"),
            P("ctx", "ch"),
            P("ctx", "ch"),
            P("ctx", "ch"),
        ),
        out_specs=(P(None, "ctx", "ch"), P(None, None, "ch"), P("ctx", "ch"), P()),
        check_vma=False,
    )
```

```python
import functools
import math

import jax
import jax.numpy as jnp
import ml_dtypes
import numpy as np
from jax import lax
from jax.experimental import pallas as pl
from jax.experimental.pallas import tpu as pltpu
from jax.sharding import PartitionSpec as P


def to_pairs(matrix, ctx_count):
    local_rows, local_channels = matrix.shape
    channel_width = local_channels // ctx_count
    shaped = matrix.reshape(local_rows // 2, 2, ctx_count, channel_width)
    return jnp.transpose(shaped, (0, 2, 1, 3)).reshape(
        local_rows // 2, ctx_count * 2 * channel_width
    )


def from_pairs(matrix, ctx_count):
    half_rows, joined = matrix.shape
    channel_width = joined // (2 * ctx_count)
    shaped = matrix.reshape(half_rows, ctx_count, 2, channel_width)
    return jnp.transpose(shaped, (0, 2, 1, 3)).reshape(half_rows * 2, ctx_count * channel_width)


def rows_down(matrix, count):
    if count == 0:
        return matrix
    filler = jnp.zeros((count, matrix.shape[1]), matrix.dtype)
    return jnp.concatenate([filler, matrix[:-count]], axis=0)


def rows_up(matrix, count):
    if count == 0:
        return matrix
    filler = jnp.zeros((count, matrix.shape[1]), matrix.dtype)
    return jnp.concatenate([matrix[count:], filler], axis=0)


def retard(matrix, offset, channel_width):
    quotient, remainder = divmod(offset, 2)
    result = rows_down(matrix, quotient)
    if remainder:
        rolled = jnp.roll(result, channel_width, axis=1)
        first_half = lax.broadcasted_iota(jnp.int32, (1, matrix.shape[1]), 1) < channel_width
        result = jnp.where(first_half, rows_down(rolled, 1), rolled)
    return result


def advance(matrix, offset, channel_width):
    quotient, remainder = divmod(offset, 2)
    result = rows_up(matrix, quotient)
    if remainder:
        rolled = jnp.roll(result, channel_width, axis=1)
        first_half = lax.broadcasted_iota(jnp.int32, (1, matrix.shape[1]), 1) < channel_width
        result = jnp.where(first_half, rolled, rows_up(rolled, 1))
    return result


def fourier_table(count, period):
    row_index = lax.broadcasted_iota(jnp.int32, (count, count), 0)
    col_index = lax.broadcasted_iota(jnp.int32, (count, count), 1)
    exponent = row_index * col_index % period
    angle = exponent.astype(jnp.float32) * (-2.0 * math.pi / period)
    return (jnp.cos(angle), jnp.sin(angle))


def angle_pair(exponent, period):
    angle = exponent.astype(jnp.float32) * (-2.0 * math.pi / period)
    return (jnp.cos(angle), jnp.sin(angle))


def contract(form, real_table, imag_table, real_part, imag_part):
    highest = lax.Precision.HIGHEST
    first = jnp.einsum(form, real_table, real_part, precision=highest) - jnp.einsum(
        form, imag_table, imag_part, precision=highest
    )
    second = jnp.einsum(form, real_table, imag_part, precision=highest) + jnp.einsum(
        form, imag_table, real_part, precision=highest
    )
    return (first, second)


def rotate(real_part, imag_part, cosine_part, sine_part):
    return (
        real_part * cosine_part - imag_part * sine_part,
        real_part * sine_part + imag_part * cosine_part,
    )


def build_tables(radix_a, radix_b, radix_c, channel_width):
    period = radix_a * radix_b * radix_c
    shape_ab = (radix_a, radix_b, 1, 1)
    digit_ka = lax.broadcasted_iota(jnp.int32, shape_ab, 0)
    digit_sb = lax.broadcasted_iota(jnp.int32, shape_ab, 1)
    turn_ab = angle_pair(radix_c * digit_sb * digit_ka % period, period)
    shape_abc = (radix_a, radix_b, radix_c, 1)
    lower_k = lax.broadcasted_iota(jnp.int32, shape_abc, 0)
    middle_k = lax.broadcasted_iota(jnp.int32, shape_abc, 1)
    digit_sc = lax.broadcasted_iota(jnp.int32, shape_abc, 2)
    turn_bc = angle_pair(digit_sc * (lower_k + radix_a * middle_k) % period, period)
    whole_k = lower_k + radix_a * middle_k + radix_a * radix_b * digit_sc
    half_cos, half_sin = angle_pair(whole_k, 2 * period)
    first_half = lax.broadcasted_iota(jnp.int32, (1, 1, 1, 2 * channel_width), 3) < channel_width
    turn_half = (jnp.where(first_half, 1.0, half_cos), jnp.where(first_half, 0.0, half_sin))
    sign_vector = jnp.where(first_half, 1.0, -1.0)
    return (
        fourier_table(radix_a, radix_a),
        fourier_table(radix_b, radix_b),
        fourier_table(radix_c, radix_c),
        turn_ab,
        turn_bc,
        turn_half,
        sign_vector,
    )


def butterfly(values, sign_vector, channel_width):
    return sign_vector * values + jnp.roll(values, channel_width, axis=3)


def forward(signal, tables, radix_a, radix_b, radix_c, channel_width):
    table_a, table_b, table_c, turn_ab, turn_bc, turn_half, sign_vector = tables
    half_a = radix_a // 2
    values = signal.astype(jnp.float32).reshape(half_a, radix_b, radix_c, 2 * channel_width)
    highest = lax.Precision.HIGHEST
    real_part = jnp.einsum("ka,abcz->kbcz", table_a[0][:, :half_a], values, precision=highest)
    imag_part = jnp.einsum("ka,abcz->kbcz", table_a[1][:, :half_a], values, precision=highest)
    real_part, imag_part = rotate(real_part, imag_part, turn_ab[0], turn_ab[1])
    real_part, imag_part = contract("kb,abcz->akcz", table_b[0], table_b[1], real_part, imag_part)
    real_part, imag_part = rotate(real_part, imag_part, turn_bc[0], turn_bc[1])
    real_part, imag_part = contract("kc,abcz->abkz", table_c[0], table_c[1], real_part, imag_part)
    real_part, imag_part = rotate(real_part, imag_part, turn_half[0], turn_half[1])
    return (
        butterfly(real_part, sign_vector, channel_width),
        butterfly(imag_part, sign_vector, channel_width),
    )


def inverse(real_part, imag_part, tables, radix_a, radix_b, radix_c, channel_width):
    table_a, table_b, table_c, turn_ab, turn_bc, turn_half, sign_vector = tables
    half_a = radix_a // 2
    real_part = butterfly(real_part, sign_vector, channel_width)
    imag_part = butterfly(imag_part, sign_vector, channel_width)
    real_part, imag_part = rotate(real_part, imag_part, turn_half[0], -turn_half[1])
    real_part, imag_part = contract("kc,abcz->abkz", table_c[0], -table_c[1], real_part, imag_part)
    real_part, imag_part = rotate(real_part, imag_part, turn_bc[0], -turn_bc[1])
    real_part, imag_part = contract("kb,abcz->akcz", table_b[0], -table_b[1], real_part, imag_part)
    real_part, imag_part = rotate(real_part, imag_part, turn_ab[0], -turn_ab[1])
    real_part, imag_part = contract(
        "ka,abcz->kbcz", table_a[0][:half_a, :], -table_a[1][:half_a, :], real_part, imag_part
    )
    half_rows = half_a * radix_b * radix_c
    return (
        real_part.reshape(half_rows, 2 * channel_width),
        imag_part.reshape(half_rows, 2 * channel_width),
    )


def spectral(filter_pairs, product_u, product_g, ctx_count, local_rows):
    channel_width = filter_pairs.shape[1] // 2
    radix_b = local_rows // 16
    radix_c = 16
    sequence_length = ctx_count * local_rows
    tables = build_tables(ctx_count, radix_b, radix_c, channel_width)
    filter_real, filter_imag = forward(
        filter_pairs, tables, ctx_count, radix_b, radix_c, channel_width
    )
    gated_real, gated_imag = forward(product_u, tables, ctx_count, radix_b, radix_c, channel_width)
    grad_real, grad_imag = forward(product_g, tables, ctx_count, radix_b, radix_c, channel_width)
    input_real = filter_real * grad_real + filter_imag * grad_imag
    input_imag = filter_real * grad_imag - filter_imag * grad_real
    lag_real = gated_real * grad_real + gated_imag * grad_imag
    lag_imag = gated_real * grad_imag - gated_imag * grad_real
    joint_real, joint_imag = inverse(
        input_real - lag_imag,
        input_imag + lag_real,
        tables,
        ctx_count,
        radix_b,
        radix_c,
        channel_width,
    )
    final_scale = 1.0 / (2.0 * sequence_length * math.sqrt(sequence_length))
    return ((joint_real * final_scale).astype(jnp.bfloat16), joint_imag * final_scale)


def shards(proj, short_filter, long_filter, out_grad, conv_out):
    ctx_count = lax.axis_size("ctx")
    local_rows, local_channels = long_filter.shape
    tap_count = short_filter.shape[1]
    channel_width = local_channels // ctx_count
    sequence_length = local_rows * ctx_count
    norm_scale = float(sequence_length) ** (-0.5)
    arrived = (
        lax.all_to_all(
            to_pairs(proj[0], ctx_count), "ctx", split_axis=1, concat_axis=0, tiled=True
        ),
        lax.all_to_all(
            to_pairs(proj[1], ctx_count), "ctx", split_axis=1, concat_axis=0, tiled=True
        ),
        lax.all_to_all(
            to_pairs(proj[2], ctx_count), "ctx", split_axis=1, concat_axis=0, tiled=True
        ),
        lax.all_to_all(
            to_pairs(long_filter, ctx_count), "ctx", split_axis=1, concat_axis=0, tiled=True
        ),
        lax.all_to_all(
            to_pairs(out_grad, ctx_count), "ctx", split_axis=1, concat_axis=0, tiled=True
        ),
        lax.all_to_all(
            to_pairs(conv_out, ctx_count), "ctx", split_axis=1, concat_axis=0, tiled=True
        ),
    )
    streams = [
        arrived[0].astype(jnp.float32),
        arrived[1].astype(jnp.float32),
        arrived[2].astype(jnp.float32),
    ]
    filter_pairs = arrived[3]
    grad_pairs = arrived[4].astype(jnp.float32)
    saved_pairs = arrived[5].astype(jnp.float32)
    local_taps = lax.dynamic_slice_in_dim(
        short_filter, lax.axis_index("ctx") * channel_width, channel_width, 2
    )
    local_taps = jnp.concatenate([local_taps, local_taps], axis=2)
    delayed = [
        [retard(streams[stream], offset, channel_width) for offset in range(tap_count)]
        for stream in range(3)
    ]
    mixed = []
    for stream in range(3):
        running = local_taps[stream, 0][None, :] * delayed[stream][0]
        for offset in range(1, tap_count):
            running = running + local_taps[stream, offset][None, :] * delayed[stream][offset]
        mixed.append(running)
    product_u = (mixed[1] * mixed[2]).astype(jnp.bfloat16)
    product_g = (grad_pairs * mixed[0]).astype(jnp.bfloat16)
    input_pairs, lag_pairs = spectral(filter_pairs, product_u, product_g, ctx_count, local_rows)
    input_values = input_pairs.astype(jnp.float32)
    stream_grads = [grad_pairs * saved_pairs, input_values * mixed[2], input_values * mixed[1]]
    outgoing = []
    tap_sums = []
    for stream in range(3):
        running = local_taps[stream, 0][None, :] * stream_grads[stream]
        for offset in range(1, tap_count):
            running = running + local_taps[stream, offset][None, :] * advance(
                stream_grads[stream], offset, channel_width
            )
        outgoing.append(running.astype(jnp.bfloat16))
        column_sums = []
        for offset in range(tap_count):
            column_total = jnp.sum(stream_grads[stream] * delayed[stream][offset], axis=0)
            column_sums.append(column_total[:channel_width] + column_total[channel_width:])
        tap_sums.append(jnp.stack(column_sums))
    returned = (
        lax.all_to_all(outgoing[0], "ctx", split_axis=0, concat_axis=1, tiled=True),
        lax.all_to_all(outgoing[1], "ctx", split_axis=0, concat_axis=1, tiled=True),
        lax.all_to_all(outgoing[2], "ctx", split_axis=0, concat_axis=1, tiled=True),
    )
    proj_grad = jnp.stack(
        [
            from_pairs(returned[0], ctx_count),
            from_pairs(returned[1], ctx_count),
            from_pairs(returned[2], ctx_count),
        ]
    )
    short_grad = lax.all_gather(jnp.stack(tap_sums), "ctx", axis=2, tiled=True) * norm_scale
    filter_grad = from_pairs(
        lax.all_to_all(lag_pairs, "ctx", split_axis=0, concat_axis=1, tiled=True), ctx_count
    )
    square_total = lax.psum(jnp.sum(filter_grad * filter_grad), ("ctx", "ch"))
    grad_square = square_total / float(sequence_length * local_channels * lax.axis_size("ch"))
    return (proj_grad, short_grad, filter_grad, grad_square)


LANES = 128
HALO = 8
MESH = pl.DeviceIdType.MESH
H, G, U, DU, LAG, PART, FINAL, SQUARE = range(8)


def real_tables(length):
    period = 2 * length
    k = np.arange(length, dtype=np.int64)[:, None]
    t = np.arange(length, dtype=np.int64)[None, :]
    angle = (k * t % period) * (2.0 * np.pi / period)
    sine = np.sin(angle)
    sine[0] = 1.0 - 2.0 * (np.arange(length) % 2)
    table = np.concatenate([np.cos(angle), sine], axis=0)
    return table.astype(ml_dtypes.bfloat16), np.ascontiguousarray(table.T).astype(ml_dtypes.bfloat16)


def fused_kernel(
    n,
    heads,
    proj_hbm,
    taps_hbm,
    long_filter,
    out_grad_hbm,
    conv_out_hbm,
    table_hbm,
    inverse_hbm,
    proj_grad,
    short_grad,
    filter_grad,
    square,
    proj,
    taps,
    out_grad,
    conv_out,
    table,
    inverse,
    halo_down,
    halo_up,
    from_prev,
    from_next,
    ext,
    mixed,
    gate,
    send_g,
    send_u,
    got_h,
    got_g,
    got_u,
    spectrum,
    product,
    du_all,
    lag_all,
    got_du,
    got_lag,
    part,
    got_part,
    final,
    got_final,
    total_ctx,
    got_ctx,
    total_ch,
    got_ch,
    send_sem,
    recv_sem,
    halo_sem,
    head_sem,
    table_sem,
):
    me = lax.axis_index("ctx")
    head = lax.axis_index("ch")
    rows = long_filter.shape[0]
    length = n * rows
    taps_count = taps.shape[1]
    norm = float(length) ** -0.5
    prev, following = lax.rem(me + n - 1, n), lax.rem(me + 1, n)

    def lanes(index):
        return pl.ds(pl.multiple_of(index * LANES, LANES), LANES)

    def block(index, size=rows):
        return pl.ds(pl.multiple_of(index * rows, rows), size)

    def send(kind, peer, source, target):
        return pltpu.make_async_remote_copy(
            src_ref=source,
            dst_ref=target,
            send_sem=send_sem.at[kind, peer],
            recv_sem=recv_sem.at[kind, me],
            device_id=(peer, head),
            device_id_type=MESH,
        )

    def arrive(kind, peer, target):
        pltpu.make_async_remote_copy(
            src_ref=target,
            dst_ref=target,
            send_sem=send_sem.at[kind, peer],
            recv_sem=recv_sem.at[kind, peer],
            device_id=(peer, head),
            device_id_type=MESH,
        ).wait_recv()

    def peers(body):
        def step(i, carry):
            body(lax.rem(me + i, n))
            return carry

        lax.fori_loop(1, n, step, 0)

    load_table = pltpu.make_async_copy(table_hbm, table, table_sem.at[0])
    load_inverse = pltpu.make_async_copy(inverse_hbm, inverse, table_sem.at[1])
    loads = [
        pltpu.make_async_copy(proj_hbm, proj, table_sem.at[2]),
        pltpu.make_async_copy(out_grad_hbm, out_grad, table_sem.at[3]),
        pltpu.make_async_copy(conv_out_hbm, conv_out, table_sem.at[4]),
        pltpu.make_async_copy(taps_hbm, taps, table_sem.at[5]),
    ]
    for load in loads:
        load.start()
    own_filter = pltpu.make_async_copy(
        long_filter.at[:, lanes(me)], got_h.at[block(me), :], table_sem.at[6]
    )
    own_filter.start()

    barrier = pltpu.get_barrier_semaphore()
    for i in range(1, n):
        pl.semaphore_signal(
            barrier, inc=1, device_id=(lax.rem(me + i, n), head), device_id_type=MESH
        )
    for i in range(1, heads):
        pl.semaphore_signal(
            barrier, inc=1, device_id=(me, lax.rem(head + i, heads)), device_id_type=MESH
        )

    for load in loads:
        load.wait()
    load_table.start()
    load_inverse.start()
    row = lax.broadcasted_iota(jnp.int32, (16, proj.shape[2]), 0)

    def pack(parts):
        packed = jnp.zeros(row.shape, jnp.float32)
        for place, (values, first) in enumerate(parts):
            shift = (2 * place - first) % 16
            moved = pltpu.roll(values.astype(jnp.float32), shift, 0) if shift else values.astype(jnp.float32)
            packed = jnp.where((row >= 2 * place) & (row < 2 * place + 2), moved, packed)
        return packed.astype(jnp.bfloat16)

    halo_down[...] = pack([(proj[j, rows - 16 : rows, :], 14) for j in range(3)])
    halo_up[...] = pack(
        [(proj[j, 0:16, :], 0) for j in range(3)] + [(out_grad[0:16, :], 0), (conv_out[0:16, :], 0)]
    )
    pl.semaphore_wait(barrier, n - 1 + heads - 1)

    def halo(source, target, index, peer):
        return pltpu.make_async_remote_copy(
            src_ref=source,
            dst_ref=target,
            send_sem=halo_sem.at[0, index],
            recv_sem=halo_sem.at[1, index],
            device_id=(peer, head),
            device_id_type=MESH,
        )

    down = halo(halo_down, from_prev, 0, following)
    up = halo(halo_up, from_next, 1, prev)
    down.start()
    up.start()

    def send_filter(peer):
        return send(H, peer, long_filter.at[:, lanes(peer)], got_h.at[block(me), :])

    peers(lambda peer: send_filter(peer).start())
    part[...] = jnp.zeros_like(part)
    du_all[length : length + 16, :] = jnp.zeros((16, LANES), jnp.bfloat16)
    for j in range(3):
        ext[j, HALO : HALO + rows, :] = proj[j].astype(jnp.float32)
    ext[3, 0:rows, :] = out_grad[...].astype(jnp.float32) * conv_out[...].astype(jnp.float32)

    down.wait_recv()
    up.wait_recv()
    before = jnp.where(me == 0, 0.0, from_prev[...].astype(jnp.float32))
    after = jnp.where(me == n - 1, 0.0, from_next[...].astype(jnp.float32))
    for j in range(3):
        ext[j, 0:HALO, :] = pltpu.roll(before, (6 - 2 * j) % 16, 0)[0:8, :]
        ext[j, HALO + rows : 2 * HALO + rows, :] = (pltpu.roll(after, 16 - 2 * j, 0) if j else after)[0:8, :]
    ext[3, rows : rows + HALO, :] = (
        pltpu.roll(after, 10, 0)[0:8, :] * pltpu.roll(after, 8, 0)[0:8, :]
    )

    def gates(peer):
        at = lanes(peer)
        values = []
        for j in range(3):
            running = taps[j, 0:1, at] * ext[j, HALO : 2 * HALO + rows, at]
            for m in range(1, taps_count):
                running = running + taps[j, m : m + 1, at] * ext[j, HALO - m : 2 * HALO + rows - m, at]
            values.append(running)
        mixed[0, :, at] = values[1]
        mixed[1, :, at] = values[2]
        u = (values[1][:rows] * values[2][:rows]).astype(jnp.bfloat16)
        g = (out_grad[:, at].astype(jnp.float32) * values[0][:rows]).astype(jnp.bfloat16)
        return g, u

    def send_grad(peer):
        return send(G, peer, send_g.at[peer], got_g.at[block(me), :])

    def send_input(peer):
        return send(U, peer, send_u.at[peer], got_u.at[block(me), :])

    def gate_peer(peer):
        g, u = gates(peer)
        send_g[peer] = g
        send_u[peer] = u
        send_grad(peer).start()

    peers(gate_peer)
    peers(lambda peer: send_input(peer).start())
    g, u = gates(me)
    got_g[block(me), :] = g
    got_u[block(me), :] = u

    def stream(j, at, index, read):
        running = taps[j, 0:1, at] * read(0)
        for m in range(1, taps_count):
            running = running + taps[j, m : m + 1, at] * read(m)
        proj_grad[j, :, at] = running.astype(jnp.bfloat16)
        for m in range(taps_count):
            part[index, j * taps_count + m : j * taps_count + m + 1, :] = jnp.sum(
                read(0) * ext[j, HALO - m : HALO + rows - m, at], axis=0, keepdims=True
            )

    def first_stream(index, carry):
        at = lanes(index)
        stream(0, at, index, lambda m: ext[3, m : m + rows, at])
        return carry

    lax.fori_loop(0, n, first_stream, 0)

    step_rows = min(1024, length)

    def transform(slot, source):
        def tile(i, carry):
            at = pl.ds(pl.multiple_of(i * step_rows, step_rows), step_rows)
            spectrum[slot, at, :] = jnp.dot(
                table[at, :], source[...], preferred_element_type=jnp.float32
            )
            return carry

        lax.fori_loop(0, 2 * length // step_rows, tile, 0)

    def correlate(slot):
        def tile(i, carry):
            low = pl.ds(pl.multiple_of(i * step_rows, step_rows), step_rows)
            high = pl.ds(pl.multiple_of(length + i * step_rows, step_rows), step_rows)
            a_cos, a_sin = spectrum[slot, low, :], spectrum[slot, high, :]
            g_cos, g_sin = spectrum[1, low, :], spectrum[1, high, :]
            edge = lax.broadcasted_iota(jnp.int32, (step_rows, LANES), 0) + i * step_rows == 0
            cos_cos, sin_sin = a_cos * g_cos, a_sin * g_sin
            product[low, :] = jnp.where(edge, 0.5 * cos_cos, cos_cos + sin_sin).astype(jnp.bfloat16)
            product[high, :] = jnp.where(
                edge, 0.5 * sin_sin, a_cos * g_sin - a_sin * g_cos
            ).astype(jnp.bfloat16)
            return carry

        lax.fori_loop(0, length // step_rows, tile, 0)

    def invert(store, start):
        def tile(i, carry):
            at = pl.ds(pl.multiple_of(i * step_rows, step_rows), step_rows)
            values = jnp.dot(inverse[at, :], product[...], preferred_element_type=jnp.float32)
            return store(at, values * (norm / length), carry)

        return lax.fori_loop(0, length // step_rows, tile, start)

    load_table.wait()
    own_filter.wait()
    peers(lambda peer: arrive(H, peer, got_h.at[block(peer), :]))
    transform(0, got_h)
    peers(lambda peer: arrive(G, peer, got_g.at[block(peer), :]))
    transform(1, got_g)
    correlate(0)
    load_inverse.wait()

    def store_du(at, values, carry):
        du_all[at, :] = values.astype(jnp.bfloat16)
        return carry

    invert(store_du, 0)

    def send_du(peer):
        return send(DU, peer, du_all.at[block(peer, rows + 16), :], got_du.at[me])

    peers(lambda peer: send_du(peer).start())
    got_du[me] = du_all[block(me, rows + 16), :]

    peers(lambda peer: arrive(U, peer, got_u.at[block(peer), :]))
    transform(2, got_u)
    correlate(2)

    def store_lag(at, values, carry):
        lag_all[at, :] = values.astype(jnp.bfloat16)
        return carry + jnp.sum((values * values).reshape(step_rows // 8, 8, LANES), axis=0)

    total_ctx[...] = invert(store_lag, jnp.zeros((8, LANES), jnp.float32))

    def send_square(peer):
        return send(SQUARE, peer, total_ctx, got_ctx.at[me])

    def send_lag(peer):
        return send(LAG, peer, lag_all.at[block(peer), :], got_lag.at[me])

    peers(lambda peer: send_square(peer).start())
    peers(lambda peer: send_lag(peer).start())

    def send_part(peer):
        return send(PART, peer, part.at[peer], got_part.at[me])

    def rest(index):
        at = lanes(index)
        du = got_du[index].astype(jnp.float32)[: rows + HALO]
        gate[0] = du * mixed[1, :, at]
        gate[1] = du * mixed[0, :, at]
        stream(1, at, index, lambda m: gate[0, m : m + rows, :])
        stream(2, at, index, lambda m: gate[1, m : m + rows, :])

    def rest_peer(peer):
        arrive(DU, peer, got_du.at[peer])
        rest(peer)
        send_part(peer).start()

    rest(me)
    peers(rest_peer)

    total = total_ctx[...]
    for i in range(1, n):
        peer = lax.rem(me + i, n)
        arrive(SQUARE, peer, got_ctx.at[peer])
        total = total + got_ctx[peer]
    total_ch[...] = total

    def send_head(i):
        return pltpu.make_async_remote_copy(
            src_ref=total_ch,
            dst_ref=got_ch.at[i],
            send_sem=head_sem.at[0, i],
            recv_sem=head_sem.at[1, i],
            device_id=(me, lax.rem(head + i, heads)),
            device_id_type=MESH,
        )

    for i in range(1, heads):
        send_head(i).start()

    sums = part[me]
    for i in range(1, n):
        peer = lax.rem(me + i, n)
        arrive(PART, peer, got_part.at[peer])
        sums = sums + got_part[peer]
    final[...] = sums * norm
    got_final[me] = sums * norm

    def send_final(peer):
        return send(FINAL, peer, final, got_final.at[me])

    peers(lambda peer: send_final(peer).start())

    filter_grad[:, lanes(me)] = lag_all[block(me), :].astype(jnp.float32)

    def take_lag(peer):
        arrive(LAG, peer, got_lag.at[peer])
        filter_grad[:, lanes(peer)] = got_lag[peer].astype(jnp.float32)

    peers(take_lag)

    total = total_ch[...]
    for i in range(1, heads):
        send_head(i).wait_recv()
        total = total + got_ch[i]
    square[...] = jnp.broadcast_to(
        jnp.sum(total, keepdims=True) / float(length * n * LANES * heads), square.shape
    )

    def put_final(index):
        at = lanes(index)
        for j in range(3):
            for m in range(taps_count):
                place = j * taps_count + m
                short_grad[j, m : m + 1, at] = got_final[index, place : place + 1, :]

    def take_final(peer):
        arrive(FINAL, peer, got_final.at[peer])
        put_final(peer)

    put_final(me)
    peers(take_final)

    down.wait_send()
    up.wait_send()
    for i in range(1, heads):
        send_head(i).wait_send()

    def sent(peer):
        for one in (
            send_filter,
            send_grad,
            send_input,
            send_du,
            send_square,
            send_lag,
            send_part,
            send_final,
        ):
            one(peer).wait_send()

    peers(sent)


def fused_shards(tables, proj, short_filter, long_filter, out_grad, conv_out):
    n = lax.axis_size("ctx")
    heads = lax.axis_size("ch")
    rows, channels = long_filter.shape
    length = n * rows
    bf16, f32 = jnp.bfloat16, jnp.float32
    vmem = pl.BlockSpec(memory_space=pltpu.VMEM)
    hbm = pl.BlockSpec(memory_space=pltpu.HBM)
    outs = pl.pallas_call(
        functools.partial(fused_kernel, n, heads),
        out_shape=(
            pltpu.VMEM((3, rows, channels), bf16),
            pltpu.VMEM(short_filter.shape, f32),
            pltpu.VMEM((rows, channels), f32),
            pltpu.VMEM((8, LANES), f32),
        ),
        in_specs=[hbm] * 7,
        out_specs=(vmem,) * 4,
        scratch_shapes=[
            pltpu.VMEM((3, rows, channels), bf16),
            pltpu.VMEM(short_filter.shape, f32),
            pltpu.VMEM((rows, channels), bf16),
            pltpu.VMEM((rows, channels), bf16),
            pltpu.VMEM((2 * length, length), bf16),
            pltpu.VMEM((length, 2 * length), bf16),
            pltpu.VMEM((16, channels), bf16),
            pltpu.VMEM((16, channels), bf16),
            pltpu.VMEM((16, channels), bf16),
            pltpu.VMEM((16, channels), bf16),
            pltpu.VMEM((4, rows + 2 * HALO, channels), f32),
            pltpu.VMEM((2, rows + HALO, channels), f32),
            pltpu.VMEM((2, rows + HALO, LANES), f32),
            pltpu.VMEM((n, rows, LANES), bf16),
            pltpu.VMEM((n, rows, LANES), bf16),
            pltpu.VMEM((length, LANES), bf16),
            pltpu.VMEM((length, LANES), bf16),
            pltpu.VMEM((length, LANES), bf16),
            pltpu.VMEM((3, 2 * length, LANES), f32),
            pltpu.VMEM((2 * length, LANES), bf16),
            pltpu.VMEM((length + 16, LANES), bf16),
            pltpu.VMEM((length, LANES), bf16),
            pltpu.VMEM((n, rows + 16, LANES), bf16),
            pltpu.VMEM((n, rows, LANES), bf16),
            pltpu.VMEM((n, 16, LANES), f32),
            pltpu.VMEM((n, 16, LANES), f32),
            pltpu.VMEM((16, LANES), f32),
            pltpu.VMEM((n, 16, LANES), f32),
            pltpu.VMEM((8, LANES), f32),
            pltpu.VMEM((n, 8, LANES), f32),
            pltpu.VMEM((8, LANES), f32),
            pltpu.VMEM((heads, 8, LANES), f32),
            pltpu.SemaphoreType.DMA((8, n)),
            pltpu.SemaphoreType.DMA((8, n)),
            pltpu.SemaphoreType.DMA((2, 2)),
            pltpu.SemaphoreType.DMA((2, heads)),
            pltpu.SemaphoreType.DMA((7,)),
        ],
        compiler_params=pltpu.CompilerParams(
            collective_id=0, has_side_effects=True, vmem_limit_bytes=54 * 1024 * 1024
        ),
    )(proj, short_filter, long_filter, out_grad, conv_out, *tables)
    return (outs[0], outs[1], outs[2], outs[3][0, 0])


def program(proj, short_filter, long_filter, out_grad, conv_out):
    n = lax.axis_size("ctx")
    rows, channels = long_filter.shape
    length = n * rows
    fits = (
        channels == n * LANES
        and length in (256, 512, 1024)
        and rows % 16 == 0
        and n > 2
        and short_filter.shape[1] == 3
    )
    if not fits:
        return shards(proj, short_filter, long_filter, out_grad, conv_out)
    tables = [jnp.asarray(one) for one in real_tables(length)]
    return fused_shards(tables, proj, short_filter, long_filter, out_grad, conv_out)


def solution(mesh):
    return jax.shard_map(
        program,
        mesh=mesh,
        in_specs=(
            P(None, "ctx", "ch"),
            P(None, None, "ch"),
            P("ctx", "ch"),
            P("ctx", "ch"),
            P("ctx", "ch"),
        ),
        out_specs=(P(None, "ctx", "ch"), P(None, None, "ch"), P("ctx", "ch"), P()),
        check_vma=False,
    )
```

```python
import functools
import math

import jax
import jax.numpy as jnp
import ml_dtypes
import numpy as np
from jax import lax
from jax.experimental import pallas as pl
from jax.experimental.pallas import tpu as pltpu
from jax.sharding import PartitionSpec as P


def to_pairs(matrix, ctx_count):
    local_rows, local_channels = matrix.shape
    channel_width = local_channels // ctx_count
    shaped = matrix.reshape(local_rows // 2, 2, ctx_count, channel_width)
    return jnp.transpose(shaped, (0, 2, 1, 3)).reshape(
        local_rows // 2, ctx_count * 2 * channel_width
    )


def from_pairs(matrix, ctx_count):
    half_rows, joined = matrix.shape
    channel_width = joined // (2 * ctx_count)
    shaped = matrix.reshape(half_rows, ctx_count, 2, channel_width)
    return jnp.transpose(shaped, (0, 2, 1, 3)).reshape(half_rows * 2, ctx_count * channel_width)


def rows_down(matrix, count):
    if count == 0:
        return matrix
    filler = jnp.zeros((count, matrix.shape[1]), matrix.dtype)
    return jnp.concatenate([filler, matrix[:-count]], axis=0)


def rows_up(matrix, count):
    if count == 0:
        return matrix
    filler = jnp.zeros((count, matrix.shape[1]), matrix.dtype)
    return jnp.concatenate([matrix[count:], filler], axis=0)


def retard(matrix, offset, channel_width):
    quotient, remainder = divmod(offset, 2)
    result = rows_down(matrix, quotient)
    if remainder:
        rolled = jnp.roll(result, channel_width, axis=1)
        first_half = lax.broadcasted_iota(jnp.int32, (1, matrix.shape[1]), 1) < channel_width
        result = jnp.where(first_half, rows_down(rolled, 1), rolled)
    return result


def advance(matrix, offset, channel_width):
    quotient, remainder = divmod(offset, 2)
    result = rows_up(matrix, quotient)
    if remainder:
        rolled = jnp.roll(result, channel_width, axis=1)
        first_half = lax.broadcasted_iota(jnp.int32, (1, matrix.shape[1]), 1) < channel_width
        result = jnp.where(first_half, rolled, rows_up(rolled, 1))
    return result


def fourier_table(count, period):
    row_index = lax.broadcasted_iota(jnp.int32, (count, count), 0)
    col_index = lax.broadcasted_iota(jnp.int32, (count, count), 1)
    exponent = row_index * col_index % period
    angle = exponent.astype(jnp.float32) * (-2.0 * math.pi / period)
    return (jnp.cos(angle), jnp.sin(angle))


def angle_pair(exponent, period):
    angle = exponent.astype(jnp.float32) * (-2.0 * math.pi / period)
    return (jnp.cos(angle), jnp.sin(angle))


def contract(form, real_table, imag_table, real_part, imag_part):
    highest = lax.Precision.HIGHEST
    first = jnp.einsum(form, real_table, real_part, precision=highest) - jnp.einsum(
        form, imag_table, imag_part, precision=highest
    )
    second = jnp.einsum(form, real_table, imag_part, precision=highest) + jnp.einsum(
        form, imag_table, real_part, precision=highest
    )
    return (first, second)


def rotate(real_part, imag_part, cosine_part, sine_part):
    return (
        real_part * cosine_part - imag_part * sine_part,
        real_part * sine_part + imag_part * cosine_part,
    )


def build_tables(radix_a, radix_b, radix_c, channel_width):
    period = radix_a * radix_b * radix_c
    shape_ab = (radix_a, radix_b, 1, 1)
    digit_ka = lax.broadcasted_iota(jnp.int32, shape_ab, 0)
    digit_sb = lax.broadcasted_iota(jnp.int32, shape_ab, 1)
    turn_ab = angle_pair(radix_c * digit_sb * digit_ka % period, period)
    shape_abc = (radix_a, radix_b, radix_c, 1)
    lower_k = lax.broadcasted_iota(jnp.int32, shape_abc, 0)
    middle_k = lax.broadcasted_iota(jnp.int32, shape_abc, 1)
    digit_sc = lax.broadcasted_iota(jnp.int32, shape_abc, 2)
    turn_bc = angle_pair(digit_sc * (lower_k + radix_a * middle_k) % period, period)
    whole_k = lower_k + radix_a * middle_k + radix_a * radix_b * digit_sc
    half_cos, half_sin = angle_pair(whole_k, 2 * period)
    first_half = lax.broadcasted_iota(jnp.int32, (1, 1, 1, 2 * channel_width), 3) < channel_width
    turn_half = (jnp.where(first_half, 1.0, half_cos), jnp.where(first_half, 0.0, half_sin))
    sign_vector = jnp.where(first_half, 1.0, -1.0)
    return (
        fourier_table(radix_a, radix_a),
        fourier_table(radix_b, radix_b),
        fourier_table(radix_c, radix_c),
        turn_ab,
        turn_bc,
        turn_half,
        sign_vector,
    )


def butterfly(values, sign_vector, channel_width):
    return sign_vector * values + jnp.roll(values, channel_width, axis=3)


def forward(signal, tables, radix_a, radix_b, radix_c, channel_width):
    table_a, table_b, table_c, turn_ab, turn_bc, turn_half, sign_vector = tables
    half_a = radix_a // 2
    values = signal.astype(jnp.float32).reshape(half_a, radix_b, radix_c, 2 * channel_width)
    highest = lax.Precision.HIGHEST
    real_part = jnp.einsum("ka,abcz->kbcz", table_a[0][:, :half_a], values, precision=highest)
    imag_part = jnp.einsum("ka,abcz->kbcz", table_a[1][:, :half_a], values, precision=highest)
    real_part, imag_part = rotate(real_part, imag_part, turn_ab[0], turn_ab[1])
    real_part, imag_part = contract("kb,abcz->akcz", table_b[0], table_b[1], real_part, imag_part)
    real_part, imag_part = rotate(real_part, imag_part, turn_bc[0], turn_bc[1])
    real_part, imag_part = contract("kc,abcz->abkz", table_c[0], table_c[1], real_part, imag_part)
    real_part, imag_part = rotate(real_part, imag_part, turn_half[0], turn_half[1])
    return (
        butterfly(real_part, sign_vector, channel_width),
        butterfly(imag_part, sign_vector, channel_width),
    )


def inverse(real_part, imag_part, tables, radix_a, radix_b, radix_c, channel_width):
    table_a, table_b, table_c, turn_ab, turn_bc, turn_half, sign_vector = tables
    half_a = radix_a // 2
    real_part = butterfly(real_part, sign_vector, channel_width)
    imag_part = butterfly(imag_part, sign_vector, channel_width)
    real_part, imag_part = rotate(real_part, imag_part, turn_half[0], -turn_half[1])
    real_part, imag_part = contract("kc,abcz->abkz", table_c[0], -table_c[1], real_part, imag_part)
    real_part, imag_part = rotate(real_part, imag_part, turn_bc[0], -turn_bc[1])
    real_part, imag_part = contract("kb,abcz->akcz", table_b[0], -table_b[1], real_part, imag_part)
    real_part, imag_part = rotate(real_part, imag_part, turn_ab[0], -turn_ab[1])
    real_part, imag_part = contract(
        "ka,abcz->kbcz", table_a[0][:half_a, :], -table_a[1][:half_a, :], real_part, imag_part
    )
    half_rows = half_a * radix_b * radix_c
    return (
        real_part.reshape(half_rows, 2 * channel_width),
        imag_part.reshape(half_rows, 2 * channel_width),
    )


def spectral(filter_pairs, product_u, product_g, ctx_count, local_rows):
    channel_width = filter_pairs.shape[1] // 2
    radix_b = local_rows // 16
    radix_c = 16
    sequence_length = ctx_count * local_rows
    tables = build_tables(ctx_count, radix_b, radix_c, channel_width)
    filter_real, filter_imag = forward(
        filter_pairs, tables, ctx_count, radix_b, radix_c, channel_width
    )
    gated_real, gated_imag = forward(product_u, tables, ctx_count, radix_b, radix_c, channel_width)
    grad_real, grad_imag = forward(product_g, tables, ctx_count, radix_b, radix_c, channel_width)
    input_real = filter_real * grad_real + filter_imag * grad_imag
    input_imag = filter_real * grad_imag - filter_imag * grad_real
    lag_real = gated_real * grad_real + gated_imag * grad_imag
    lag_imag = gated_real * grad_imag - gated_imag * grad_real
    joint_real, joint_imag = inverse(
        input_real - lag_imag,
        input_imag + lag_real,
        tables,
        ctx_count,
        radix_b,
        radix_c,
        channel_width,
    )
    final_scale = 1.0 / (2.0 * sequence_length * math.sqrt(sequence_length))
    return ((joint_real * final_scale).astype(jnp.bfloat16), joint_imag * final_scale)


def shards(proj, short_filter, long_filter, out_grad, conv_out):
    ctx_count = lax.axis_size("ctx")
    local_rows, local_channels = long_filter.shape
    tap_count = short_filter.shape[1]
    channel_width = local_channels // ctx_count
    sequence_length = local_rows * ctx_count
    norm_scale = float(sequence_length) ** (-0.5)
    arrived = (
        lax.all_to_all(
            to_pairs(proj[0], ctx_count), "ctx", split_axis=1, concat_axis=0, tiled=True
        ),
        lax.all_to_all(
            to_pairs(proj[1], ctx_count), "ctx", split_axis=1, concat_axis=0, tiled=True
        ),
        lax.all_to_all(
            to_pairs(proj[2], ctx_count), "ctx", split_axis=1, concat_axis=0, tiled=True
        ),
        lax.all_to_all(
            to_pairs(long_filter, ctx_count), "ctx", split_axis=1, concat_axis=0, tiled=True
        ),
        lax.all_to_all(
            to_pairs(out_grad, ctx_count), "ctx", split_axis=1, concat_axis=0, tiled=True
        ),
        lax.all_to_all(
            to_pairs(conv_out, ctx_count), "ctx", split_axis=1, concat_axis=0, tiled=True
        ),
    )
    streams = [
        arrived[0].astype(jnp.float32),
        arrived[1].astype(jnp.float32),
        arrived[2].astype(jnp.float32),
    ]
    filter_pairs = arrived[3]
    grad_pairs = arrived[4].astype(jnp.float32)
    saved_pairs = arrived[5].astype(jnp.float32)
    local_taps = lax.dynamic_slice_in_dim(
        short_filter, lax.axis_index("ctx") * channel_width, channel_width, 2
    )
    local_taps = jnp.concatenate([local_taps, local_taps], axis=2)
    delayed = [
        [retard(streams[stream], offset, channel_width) for offset in range(tap_count)]
        for stream in range(3)
    ]
    mixed = []
    for stream in range(3):
        running = local_taps[stream, 0][None, :] * delayed[stream][0]
        for offset in range(1, tap_count):
            running = running + local_taps[stream, offset][None, :] * delayed[stream][offset]
        mixed.append(running)
    product_u = (mixed[1] * mixed[2]).astype(jnp.bfloat16)
    product_g = (grad_pairs * mixed[0]).astype(jnp.bfloat16)
    input_pairs, lag_pairs = spectral(filter_pairs, product_u, product_g, ctx_count, local_rows)
    input_values = input_pairs.astype(jnp.float32)
    stream_grads = [grad_pairs * saved_pairs, input_values * mixed[2], input_values * mixed[1]]
    outgoing = []
    tap_sums = []
    for stream in range(3):
        running = local_taps[stream, 0][None, :] * stream_grads[stream]
        for offset in range(1, tap_count):
            running = running + local_taps[stream, offset][None, :] * advance(
                stream_grads[stream], offset, channel_width
            )
        outgoing.append(running.astype(jnp.bfloat16))
        column_sums = []
        for offset in range(tap_count):
            column_total = jnp.sum(stream_grads[stream] * delayed[stream][offset], axis=0)
            column_sums.append(column_total[:channel_width] + column_total[channel_width:])
        tap_sums.append(jnp.stack(column_sums))
    returned = (
        lax.all_to_all(outgoing[0], "ctx", split_axis=0, concat_axis=1, tiled=True),
        lax.all_to_all(outgoing[1], "ctx", split_axis=0, concat_axis=1, tiled=True),
        lax.all_to_all(outgoing[2], "ctx", split_axis=0, concat_axis=1, tiled=True),
    )
    proj_grad = jnp.stack(
        [
            from_pairs(returned[0], ctx_count),
            from_pairs(returned[1], ctx_count),
            from_pairs(returned[2], ctx_count),
        ]
    )
    short_grad = lax.all_gather(jnp.stack(tap_sums), "ctx", axis=2, tiled=True) * norm_scale
    filter_grad = from_pairs(
        lax.all_to_all(lag_pairs, "ctx", split_axis=0, concat_axis=1, tiled=True), ctx_count
    )
    square_total = lax.psum(jnp.sum(filter_grad * filter_grad), ("ctx", "ch"))
    grad_square = square_total / float(sequence_length * local_channels * lax.axis_size("ch"))
    return (proj_grad, short_grad, filter_grad, grad_square)


LANES = 128
HALO = 8
MESH = pl.DeviceIdType.MESH
H, G, U, DU, LAG, PART, FINAL = range(7)


def real_tables(length):
    period = 2 * length
    k = np.arange(length, dtype=np.int64)[:, None]
    t = np.arange(length, dtype=np.int64)[None, :]
    angle = (k * t % period) * (2.0 * np.pi / period)
    sine = np.sin(angle)
    sine[0] = 1.0 - 2.0 * (np.arange(length) % 2)
    table = np.concatenate([np.cos(angle), sine], axis=0)
    return table.astype(ml_dtypes.bfloat16), np.ascontiguousarray(table.T).astype(ml_dtypes.bfloat16)


def fused_kernel(
    n,
    heads,
    proj_hbm,
    taps_hbm,
    long_filter,
    out_grad_hbm,
    conv_out_hbm,
    table_hbm,
    inverse_hbm,
    proj_grad,
    short_grad,
    filter_grad,
    square,
    proj,
    taps,
    out_grad,
    conv_out,
    table,
    inverse,
    halo_down,
    halo_up,
    from_prev,
    from_next,
    ext,
    mixed,
    gate,
    send_g,
    send_u,
    got_h,
    got_g,
    got_u,
    spectrum,
    product,
    du_all,
    lag_all,
    got_du,
    got_lag,
    part,
    part_out,
    got_part,
    final,
    got_final,
    total_ch,
    got_ch,
    send_sem,
    recv_sem,
    halo_sem,
    head_sem,
    table_sem,
):
    me = lax.axis_index("ctx")
    head = lax.axis_index("ch")
    rows = long_filter.shape[0]
    length = n * rows
    taps_count = taps.shape[1]
    norm = float(length) ** -0.5
    prev, following = lax.rem(me + n - 1, n), lax.rem(me + 1, n)

    def lanes(index):
        return pl.ds(pl.multiple_of(index * LANES, LANES), LANES)

    def block(index, size=rows):
        return pl.ds(pl.multiple_of(index * rows, rows), size)

    def send(kind, peer, source, target):
        return pltpu.make_async_remote_copy(
            src_ref=source,
            dst_ref=target,
            send_sem=send_sem.at[kind, peer],
            recv_sem=recv_sem.at[kind, me],
            device_id=(peer, head),
            device_id_type=MESH,
        )

    def arrive(kind, peer, target):
        pltpu.make_async_remote_copy(
            src_ref=target,
            dst_ref=target,
            send_sem=send_sem.at[kind, peer],
            recv_sem=recv_sem.at[kind, peer],
            device_id=(peer, head),
            device_id_type=MESH,
        ).wait_recv()

    def peers(body):
        def step(i, carry):
            body(lax.rem(me + i, n))
            return carry

        lax.fori_loop(1, n, step, 0)

    load_table = pltpu.make_async_copy(table_hbm, table, table_sem.at[0])
    load_inverse = pltpu.make_async_copy(inverse_hbm, inverse, table_sem.at[1])
    loads = [
        pltpu.make_async_copy(proj_hbm, proj, table_sem.at[2]),
        pltpu.make_async_copy(out_grad_hbm, out_grad, table_sem.at[3]),
        pltpu.make_async_copy(conv_out_hbm, conv_out, table_sem.at[4]),
        pltpu.make_async_copy(taps_hbm, taps, table_sem.at[5]),
    ]
    for load in loads:
        load.start()
    own_filter = pltpu.make_async_copy(
        long_filter.at[:, lanes(me)], got_h.at[block(me), :], table_sem.at[6]
    )
    own_filter.start()

    barrier = pltpu.get_barrier_semaphore()
    for i in range(1, n):
        pl.semaphore_signal(
            barrier, inc=1, device_id=(lax.rem(me + i, n), head), device_id_type=MESH
        )
    for i in range(1, heads):
        pl.semaphore_signal(
            barrier, inc=1, device_id=(me, lax.rem(head + i, heads)), device_id_type=MESH
        )

    for load in loads:
        load.wait()
    load_table.start()
    load_inverse.start()
    row = lax.broadcasted_iota(jnp.int32, (16, proj.shape[2]), 0)

    def pack(parts):
        packed = jnp.zeros(row.shape, jnp.float32)
        for place, (values, first) in enumerate(parts):
            shift = (2 * place - first) % 16
            moved = pltpu.roll(values.astype(jnp.float32), shift, 0) if shift else values.astype(jnp.float32)
            packed = jnp.where((row >= 2 * place) & (row < 2 * place + 2), moved, packed)
        return packed.astype(jnp.bfloat16)

    halo_down[...] = pack([(proj[j, rows - 16 : rows, :], 14) for j in range(3)])
    halo_up[...] = pack(
        [(proj[j, 0:16, :], 0) for j in range(3)] + [(out_grad[0:16, :], 0), (conv_out[0:16, :], 0)]
    )
    pl.semaphore_wait(barrier, n - 1 + heads - 1)

    def halo(source, target, index, peer):
        return pltpu.make_async_remote_copy(
            src_ref=source,
            dst_ref=target,
            send_sem=halo_sem.at[0, index],
            recv_sem=halo_sem.at[1, index],
            device_id=(peer, head),
            device_id_type=MESH,
        )

    down = halo(halo_down, from_prev, 0, following)
    up = halo(halo_up, from_next, 1, prev)
    down.start()
    up.start()

    def send_filter(peer):
        return send(H, peer, long_filter.at[:, lanes(peer)], got_h.at[block(me), :])

    peers(lambda peer: send_filter(peer).start())
    part[...] = jnp.zeros_like(part)
    du_all[length : length + 16, :] = jnp.zeros((16, LANES), jnp.bfloat16)
    for j in range(3):
        ext[j, HALO : HALO + rows, :] = proj[j].astype(jnp.float32)
    ext[3, 0:rows, :] = out_grad[...].astype(jnp.float32) * conv_out[...].astype(jnp.float32)

    down.wait_recv()
    up.wait_recv()
    before = jnp.where(me == 0, 0.0, from_prev[...].astype(jnp.float32))
    after = jnp.where(me == n - 1, 0.0, from_next[...].astype(jnp.float32))
    for j in range(3):
        ext[j, 0:HALO, :] = pltpu.roll(before, (6 - 2 * j) % 16, 0)[0:8, :]
        ext[j, HALO + rows : 2 * HALO + rows, :] = (pltpu.roll(after, 16 - 2 * j, 0) if j else after)[0:8, :]
    ext[3, rows : rows + HALO, :] = (
        pltpu.roll(after, 10, 0)[0:8, :] * pltpu.roll(after, 8, 0)[0:8, :]
    )

    def gates(peer):
        at = lanes(peer)
        values = []
        for j in range(3):
            running = taps[j, 0:1, at] * ext[j, HALO : 2 * HALO + rows, at]
            for m in range(1, taps_count):
                running = running + taps[j, m : m + 1, at] * ext[j, HALO - m : 2 * HALO + rows - m, at]
            values.append(running)
        mixed[0, :, at] = values[1]
        mixed[1, :, at] = values[2]
        u = (values[1][:rows] * values[2][:rows]).astype(jnp.bfloat16)
        g = (out_grad[:, at].astype(jnp.float32) * values[0][:rows]).astype(jnp.bfloat16)
        return g, u

    def send_grad(peer):
        return send(G, peer, send_g.at[peer], got_g.at[block(me), :])

    def send_input(peer):
        return send(U, peer, send_u.at[peer], got_u.at[block(me), :])

    def gate_peer(peer):
        g, u = gates(peer)
        send_g[peer] = g
        send_u[peer] = u
        send_grad(peer).start()

    peers(gate_peer)
    peers(lambda peer: send_input(peer).start())
    g, u = gates(me)
    got_g[block(me), :] = g
    got_u[block(me), :] = u

    def stream(j, at, index, read):
        running = taps[j, 0:1, at] * read(0)
        for m in range(1, taps_count):
            running = running + taps[j, m : m + 1, at] * read(m)
        proj_grad[j, :, at] = running.astype(jnp.bfloat16)
        for m in range(taps_count):
            part[index, j * taps_count + m : j * taps_count + m + 1, :] = jnp.sum(
                read(0) * ext[j, HALO - m : HALO + rows - m, at], axis=0, keepdims=True
            )

    def first_stream(index, carry):
        at = lanes(index)
        stream(0, at, index, lambda m: ext[3, m : m + rows, at])
        return carry

    lax.fori_loop(0, n, first_stream, 0)

    step_rows = min(1024, length)

    def transform(slot, source):
        def tile(i, carry):
            at = pl.ds(pl.multiple_of(i * step_rows, step_rows), step_rows)
            spectrum[slot, at, :] = jnp.dot(
                table[at, :], source[...], preferred_element_type=jnp.float32
            )
            return carry

        lax.fori_loop(0, 2 * length // step_rows, tile, 0)

    def correlate(slot):
        def tile(i, carry):
            low = pl.ds(pl.multiple_of(i * step_rows, step_rows), step_rows)
            high = pl.ds(pl.multiple_of(length + i * step_rows, step_rows), step_rows)
            a_cos, a_sin = spectrum[slot, low, :], spectrum[slot, high, :]
            g_cos, g_sin = spectrum[1, low, :], spectrum[1, high, :]
            edge = lax.broadcasted_iota(jnp.int32, (step_rows, LANES), 0) + i * step_rows == 0
            cos_cos, sin_sin = a_cos * g_cos, a_sin * g_sin
            product[low, :] = jnp.where(edge, 0.5 * cos_cos, cos_cos + sin_sin).astype(jnp.bfloat16)
            product[high, :] = jnp.where(
                edge, 0.5 * sin_sin, a_cos * g_sin - a_sin * g_cos
            ).astype(jnp.bfloat16)
            return carry

        lax.fori_loop(0, length // step_rows, tile, 0)

    def invert(store, start):
        def tile(i, carry):
            at = pl.ds(pl.multiple_of(i * step_rows, step_rows), step_rows)
            values = jnp.dot(inverse[at, :], product[...], preferred_element_type=jnp.float32)
            return store(at, values * (norm / length), carry)

        return lax.fori_loop(0, length // step_rows, tile, start)

    load_table.wait()
    own_filter.wait()
    peers(lambda peer: arrive(H, peer, got_h.at[block(peer), :]))
    transform(0, got_h)
    peers(lambda peer: arrive(G, peer, got_g.at[block(peer), :]))
    transform(1, got_g)
    correlate(0)
    load_inverse.wait()

    def store_du(at, values, carry):
        du_all[at, :] = values.astype(jnp.bfloat16)
        return carry

    invert(store_du, 0)

    def send_du(peer):
        return send(DU, peer, du_all.at[block(peer, rows + 16), :], got_du.at[me])

    peers(lambda peer: send_du(peer).start())
    got_du[me] = du_all[block(me, rows + 16), :]

    peers(lambda peer: arrive(U, peer, got_u.at[block(peer), :]))
    transform(2, got_u)
    correlate(2)

    def store_lag(at, values, carry):
        lag_all[at, :] = values.astype(jnp.bfloat16)
        return carry + jnp.sum((values * values).reshape(step_rows // 8, 8, LANES), axis=0)

    own_square = invert(store_lag, jnp.zeros((8, LANES), jnp.float32))

    def send_lag(peer):
        return send(LAG, peer, lag_all.at[block(peer), :], got_lag.at[me])

    peers(lambda peer: send_lag(peer).start())

    def send_part(peer):
        return send(PART, peer, part_out.at[peer], got_part.at[me])

    square_row = jnp.sum(own_square, axis=0, keepdims=True)

    def rest(index):
        at = lanes(index)
        du = got_du[index].astype(jnp.float32)[: rows + HALO]
        gate[0] = du * mixed[1, :, at]
        gate[1] = du * mixed[0, :, at]
        stream(1, at, index, lambda m: gate[0, m : m + rows, :])
        stream(2, at, index, lambda m: gate[1, m : m + rows, :])
        part[index, 9:10, :] = square_row
        part_out[index] = part[index].astype(jnp.bfloat16)

    def rest_peer(peer):
        arrive(DU, peer, got_du.at[peer])
        rest(peer)
        send_part(peer).start()

    rest(me)
    peers(rest_peer)

    sums = part_out[me].astype(jnp.float32)
    for i in range(1, n):
        peer = lax.rem(me + i, n)
        arrive(PART, peer, got_part.at[peer])
        sums = sums + got_part[peer].astype(jnp.float32)
    final[...] = (sums * norm).astype(jnp.bfloat16)
    got_final[me] = (sums * norm).astype(jnp.bfloat16)

    def send_final(peer):
        return send(FINAL, peer, final, got_final.at[me])

    peers(lambda peer: send_final(peer).start())
    total_ch[...] = jnp.broadcast_to(sums[9:10], total_ch.shape)

    def send_head(i):
        return pltpu.make_async_remote_copy(
            src_ref=total_ch,
            dst_ref=got_ch.at[i],
            send_sem=head_sem.at[0, i],
            recv_sem=head_sem.at[1, i],
            device_id=(me, lax.rem(head + i, heads)),
            device_id_type=MESH,
        )

    for i in range(1, heads):
        send_head(i).start()

    filter_grad[:, lanes(me)] = lag_all[block(me), :].astype(jnp.float32)

    def take_lag(peer):
        arrive(LAG, peer, got_lag.at[peer])
        filter_grad[:, lanes(peer)] = got_lag[peer].astype(jnp.float32)

    peers(take_lag)

    total = total_ch[...]
    for i in range(1, heads):
        send_head(i).wait_recv()
        total = total + got_ch[i]
    square[...] = jnp.broadcast_to(
        jnp.sum(total[0:1], keepdims=True) / float(length * n * LANES * heads), square.shape
    )

    def put_final(index):
        at = lanes(index)
        values = got_final[index].astype(jnp.float32)
        for j in range(3):
            for m in range(taps_count):
                place = j * taps_count + m
                short_grad[j, m : m + 1, at] = values[place : place + 1]

    def take_final(peer):
        arrive(FINAL, peer, got_final.at[peer])
        put_final(peer)

    put_final(me)
    peers(take_final)

    down.wait_send()
    up.wait_send()
    for i in range(1, heads):
        send_head(i).wait_send()

    def sent(peer):
        for one in (
            send_filter,
            send_grad,
            send_input,
            send_du,
            send_lag,
            send_part,
            send_final,
        ):
            one(peer).wait_send()

    peers(sent)


def fused_shards(tables, proj, short_filter, long_filter, out_grad, conv_out):
    n = lax.axis_size("ctx")
    heads = lax.axis_size("ch")
    rows, channels = long_filter.shape
    length = n * rows
    bf16, f32 = jnp.bfloat16, jnp.float32
    vmem = pl.BlockSpec(memory_space=pltpu.VMEM)
    hbm = pl.BlockSpec(memory_space=pltpu.HBM)
    outs = pl.pallas_call(
        functools.partial(fused_kernel, n, heads),
        out_shape=(
            pltpu.VMEM((3, rows, channels), bf16),
            pltpu.VMEM(short_filter.shape, f32),
            pltpu.VMEM((rows, channels), f32),
            pltpu.VMEM((8, LANES), f32),
        ),
        in_specs=[hbm] * 7,
        out_specs=(vmem,) * 4,
        scratch_shapes=[
            pltpu.VMEM((3, rows, channels), bf16),
            pltpu.VMEM(short_filter.shape, f32),
            pltpu.VMEM((rows, channels), bf16),
            pltpu.VMEM((rows, channels), bf16),
            pltpu.VMEM((2 * length, length), bf16),
            pltpu.VMEM((length, 2 * length), bf16),
            pltpu.VMEM((16, channels), bf16),
            pltpu.VMEM((16, channels), bf16),
            pltpu.VMEM((16, channels), bf16),
            pltpu.VMEM((16, channels), bf16),
            pltpu.VMEM((4, rows + 2 * HALO, channels), f32),
            pltpu.VMEM((2, rows + HALO, channels), f32),
            pltpu.VMEM((2, rows + HALO, LANES), f32),
            pltpu.VMEM((n, rows, LANES), bf16),
            pltpu.VMEM((n, rows, LANES), bf16),
            pltpu.VMEM((length, LANES), bf16),
            pltpu.VMEM((length, LANES), bf16),
            pltpu.VMEM((length, LANES), bf16),
            pltpu.VMEM((3, 2 * length, LANES), f32),
            pltpu.VMEM((2 * length, LANES), bf16),
            pltpu.VMEM((length + 16, LANES), bf16),
            pltpu.VMEM((length, LANES), bf16),
            pltpu.VMEM((n, rows + 16, LANES), bf16),
            pltpu.VMEM((n, rows, LANES), bf16),
            pltpu.VMEM((n, 16, LANES), f32),
            pltpu.VMEM((n, 16, LANES), bf16),
            pltpu.VMEM((n, 16, LANES), bf16),
            pltpu.VMEM((16, LANES), bf16),
            pltpu.VMEM((n, 16, LANES), bf16),
            pltpu.VMEM((8, LANES), f32),
            pltpu.VMEM((heads, 8, LANES), f32),
            pltpu.SemaphoreType.DMA((7, n)),
            pltpu.SemaphoreType.DMA((7, n)),
            pltpu.SemaphoreType.DMA((2, 2)),
            pltpu.SemaphoreType.DMA((2, heads)),
            pltpu.SemaphoreType.DMA((7,)),
        ],
        compiler_params=pltpu.CompilerParams(
            collective_id=0, has_side_effects=True, vmem_limit_bytes=54 * 1024 * 1024
        ),
    )(proj, short_filter, long_filter, out_grad, conv_out, *tables)
    return (outs[0], outs[1], outs[2], outs[3][0, 0])


def program(proj, short_filter, long_filter, out_grad, conv_out):
    n = lax.axis_size("ctx")
    rows, channels = long_filter.shape
    length = n * rows
    fits = (
        channels == n * LANES
        and length in (256, 512, 1024)
        and rows % 16 == 0
        and n > 2
        and short_filter.shape[1] == 3
    )
    if not fits:
        return shards(proj, short_filter, long_filter, out_grad, conv_out)
    tables = [jnp.asarray(one) for one in real_tables(length)]
    return fused_shards(tables, proj, short_filter, long_filter, out_grad, conv_out)


def solution(mesh):
    return jax.shard_map(
        program,
        mesh=mesh,
        in_specs=(
            P(None, "ctx", "ch"),
            P(None, None, "ch"),
            P("ctx", "ch"),
            P("ctx", "ch"),
            P("ctx", "ch"),
        ),
        out_specs=(P(None, "ctx", "ch"), P(None, None, "ch"), P("ctx", "ch"), P()),
        check_vma=False,
    )
```
